256 devices in a mesh: leaf: 32 (over x_lo, z, core), launch: 8 (over y, x_hi).
Axes of the slice: x: 4 (x_hi: 2, x_lo: 2; x = x_hi * 2 + x_lo), y: 4, z: 8, core: 2. Of those that a mesh axis runs over, the one named last changes fastest.
Arguments:
- right_side: bfloat16 [4, 128, 128, 1024], P(None, 'leaf', None, 'launch'), may hold values from -6 to 6
- diag_inverse: bfloat16 [4, 128, 128, 128], P(None, 'leaf'), may hold values from -0.5 to 0.5
- factors: bfloat16 [6, 128, 16, 128, 128], P(None, 'leaf', 'launch'), may hold values from -0.078125 to 0.078125
- pattern: int32 [6, 128, 16], P(None, 'leaf'), may hold values from 0 to 127
- owner_map: int32 [3, 128], replicated, may hold values from 0 to 127, each once within a row
Outputs:
- solutions: bfloat16 [4, 128, 128, 1024], P(None, 'leaf', None, 'launch')
The draws below stay inside these ranges and needn't reach their ends.
Inputs may be any that keep to these rules, and one draw needn't show every extreme that they name: `pattern`: entries name tree supernodes of the pair's lower level; one descendant may appear more than once. `owner_map`: each row is a permutation of the slots of one of the levels 0 to 2.
All inputs are finite; a program needn't handle non-finite values.
Results may differ from the reference program's by a relative error of at most 0.008.
Values may be sent and summed in bfloat16 or wider, within the bound.
A program may use at most 128 MiB of HBM per device.

```python
import jax
import jax.numpy as jnp

BLK = 128
LEVELS = 4
FAN = 16
PAIRS = 6
SUPS = 128
COLS = 1024


def touch_ends(entries, own_key, smallest, high):
    extent = entries.shape
    index_at = [jax.random.randint(jax.random.fold_in(own_key, axis), (), 0, extent[axis]) for axis in range(len(extent))]
    entries = entries.at[tuple(index_at)].set(smallest)
    longest = extent.index(max(extent))
    index_at[longest] = (index_at[longest] + 1) % extent[longest]
    return entries.at[tuple(index_at)].set(high)


def level_of(rng, shape, shards, low, largest):
    factor_of, own = 1.0, jax.random.fold_in(rng, 6)
    for axis_at, shards_of in shards:
        draws = jnp.exp(jax.random.uniform(jax.random.fold_in(own, axis_at), (shards_of,), jnp.float32, low / len(shards), largest / len(shards)))
        factor_of = factor_of * jnp.repeat(draws, shape[axis_at] // shards_of).reshape([-1 if axis == axis_at else 1 for axis in range(len(shape))])
    return factor_of


def gaussian(own_key, shape, width, most, pieces=(), dtype=jnp.bfloat16):
    result = width * jax.random.normal(own_key, shape, jnp.float32)
    if pieces:
        result = result * level_of(own_key, shape, pieces, -0.22, 0.18)
    return jnp.clip(result, -most, most).astype(dtype)


def setup_inputs(seed: int = 0) -> dict:
    key_of = jax.random.split(jax.random.key(seed), 6)
    return {
        "right_side": gaussian(key_of[0], (LEVELS, SUPS, BLK, COLS), 1.0, 6.0, ((1, 32), (3, 8))),
        "diag_inverse": gaussian(key_of[1], (LEVELS, SUPS, BLK, BLK), BLK ** -0.5, 0.5, ((1, 32),)),
        "factors": gaussian(key_of[2], (PAIRS, SUPS, FAN, BLK, BLK), (3 * FAN * BLK) ** -0.5, 0.078125, ((1, 32), (2, 8))),
        "pattern": touch_ends(jax.random.randint(key_of[3], (PAIRS, SUPS, FAN), 0, SUPS), jax.random.fold_in(key_of[3], 1), 0, SUPS - 1).astype(jnp.int32),
        "owner_map": jax.vmap(lambda own: jax.random.permutation(own, SUPS))(jax.random.split(key_of[4], (LEVELS - 1))).reshape((LEVELS - 1, SUPS)).astype(jnp.int32),
    }


def reference(right_side, diag_inverse, factors, pattern, owner_map):
    solutions = []
    for height in range(LEVELS):
        updates = jnp.zeros((SUPS, BLK, COLS), jnp.float32)
        for descend in range(height):
            pair_index = descend * (2 * LEVELS - descend - 1) // 2 + height - descend - 1
            slot_map = jnp.take(owner_map[descend], pattern[pair_index], axis=0)
            source = solutions[descend].astype(jnp.float32)
            for position in range(FAN):
                coupling = factors[pair_index, :, position].astype(jnp.float32)
                updates = updates + jnp.einsum("sij,sjc->sic", coupling, source[slot_map[:, position]])
        residue = (right_side[height].astype(jnp.float32) - updates).astype(jnp.bfloat16)
        solved = jnp.einsum("sij,sjc->sic", diag_inverse[height].astype(jnp.float32), residue.astype(jnp.float32))
        solutions.append(solved.astype(jnp.bfloat16))
    return jnp.stack(solutions)
```

```python
import jax
import jax.numpy as jnp
from jax import lax
from jax.experimental import pallas as pl
from jax.experimental.pallas import tpu as pltpu
from jax.sharding import PartitionSpec as P

LEVELS = 4
FAN = 16
SUPS = 128
OWN = 4
BLK = 128
COLS = 128
PARTS = 2
CHUNK = COLS // PARTS
PAIRS = 6
ZS = 8
YS = 4
LEAFS = 16

PAIR_ORDER = (0, 1, 3, 2, 4, 5)
X_FIRST = (2, 2, 2, 3, 2, 3)

GATHER_SEMS = 33
FACTOR_SEMS = 15
MESH = pl.DeviceIdType.MESH


def pair_of(lower, upper):
    return lower * (2 * LEVELS - lower - 1) // 2 + upper - lower - 1


def transposed_product(rows, blocks):
    return lax.dot_general(rows, blocks, (((1,), (1,)), ((), ())), preferred_element_type=jnp.float32)


def kernel(*refs):
    pattern, owner, right_side, diag, own_factors, out = refs[:6]
    solved = refs[6 : 6 + 3 * PARTS]
    (factors, pending, rhs_t, last, g_send, g_recv, f_send, f_recv, own_sem) = refs[6 + 3 * PARTS :]

    leaf = lax.axis_index("leaf")
    launch = lax.axis_index("launch")
    core, z, x_lo = leaf % 2, (leaf // 2) % ZS, leaf // LEAFS
    y, x_hi = launch // 2, launch % 2

    def leaf_at(xl, zz, k):
        return xl * LEAFS + zz * 2 + k

    def z_at(step):
        return (z + step + ZS) % ZS

    def y_at(step):
        return (y + step + YS) % YS

    z_up = (leaf_at(x_lo, z_at(1), core), launch)
    z_down = (leaf_at(x_lo, z_at(-1), core), launch)
    x_near = (leaf_at(1 - x_lo, z, core), launch)
    sibling = (leaf_at(x_lo, z, 1 - core), launch)
    x_far = (leaf, y * 2 + (1 - x_hi))
    y_up = (leaf, y_at(1) * 2 + x_hi)
    y_down = (leaf, y_at(-1) * 2 + x_hi)
    partners = (z_up, z_down, x_near, sibling, x_far, y_up, y_down)

    sends = []

    def send(src, dst, send_sem, recv_sem, device):
        copy = pltpu.make_async_remote_copy(
            src_ref=src, dst_ref=dst, send_sem=send_sem, recv_sem=recv_sem, device_id=device, device_id_type=MESH
        )
        copy.start()
        sends.append(copy)

    def arrived(dst, recv_sem, send_sem):
        pltpu.make_async_remote_copy(
            src_ref=dst, dst_ref=dst, send_sem=send_sem, recv_sem=recv_sem, device_id=sibling, device_id_type=MESH
        ).wait_recv()

    def slots(u, xl, zz, k, half=None):
        first = leaf_at(xl, zz, k) * OWN
        if half is None:
            return solved[u].at[pl.ds(first, OWN)]
        return solved[u].at[pl.ds(first + half * (OWN // 2), OWN // 2)]

    def g_put(u, ref, at, device):
        send(ref, ref, g_send.at[u, at], g_recv.at[u, at], device)

    def g_wait(u, ref, at):
        arrived(ref, g_recv.at[u, at], g_send.at[u, at])

    columns = (x_lo, 1 - x_lo)

    def ring(stream, down, step):
        return 1 + stream * 8 + down * 4 + step - 1

    def side(stream, offset):
        return 17 + stream * 8 + offset % ZS

    def spread(u, stream):
        block = slots(u, columns[stream], z, core)
        g_put(u, block, ring(stream, 0, 1), z_up)
        g_put(u, block, ring(stream, 1, 1), z_down)
        g_put(u, block, side(stream, 0), sibling)

    def gather_start(u):
        g_put(u, slots(u, x_lo, z, core), 0, x_near)
        spread(u, 0)

    def gather_step(u, step):
        if step == 0:
            g_wait(u, slots(u, 1 - x_lo, z, core), 0)
            spread(u, 1)
            return
        for stream in range(2):
            xl = columns[stream]
            if step < 4:
                for down, device in ((0, z_up), (1, z_down)):
                    offset = step if down else -step
                    block = slots(u, xl, z_at(offset), core)
                    g_wait(u, block, ring(stream, down, step))
                    onward = block if step < 3 else slots(u, xl, z_at(offset), core, down)
                    g_put(u, onward, ring(stream, down, step + 1), device)
                    g_put(u, block, side(stream, offset), sibling)
            else:
                for down in range(2):
                    g_wait(u, slots(u, xl, z_at(4), core, down), ring(stream, down, 4))
                g_put(u, slots(u, xl, z_at(4), core), side(stream, 4), sibling)

    def gather_end(u):
        for stream in range(2):
            for offset in range(ZS):
                g_wait(u, slots(u, columns[stream], z_at(offset), 1 - core), side(stream, offset))

    def held(p, yy, xh, y_first, half=None):
        cut = X_FIRST[p]
        which = pl.ds(cut, OWN - cut) if y_first else pl.ds(0, cut)
        if half is None:
            return factors.at[p, yy * 2 + xh, which]
        return factors.at[p, yy * 2 + xh, which, pl.ds(half, 1)]

    def f_put(p, src, dst, at, device):
        send(src, dst, f_send.at[p, at], f_recv.at[p, at], device)

    def f_wait(p, ref, at):
        arrived(ref, f_recv.at[p, at], f_send.at[p, at])

    def own_copy(p):
        return pltpu.make_async_copy(own_factors.at[p], factors.at[p, launch], own_sem.at[p])

    def factors_send(p):
        cut = X_FIRST[p]
        src_x, src_y = own_factors.at[p, pl.ds(0, cut)], own_factors.at[p, pl.ds(cut, OWN - cut)]
        dst_x, dst_y = held(p, y, x_hi, False), held(p, y, x_hi, True)
        f_put(p, src_x, dst_x, 0, x_far)
        f_put(p, src_x, dst_x, 1, y_up)
        f_put(p, src_x, dst_x, 2, y_down)
        f_put(p, src_y, dst_y, 7, y_up)
        f_put(p, src_y, dst_y, 8, y_down)
        f_put(p, src_y, dst_y, 11, x_far)
        own_copy(p).start()

    def factors_second(p):
        far = held(p, y, 1 - x_hi, False)
        f_wait(p, far, 0)
        f_put(p, far, far, 3, y_up)
        f_put(p, far, far, 4, y_down)
        below, above = held(p, y_at(-1), x_hi, True), held(p, y_at(1), x_hi, True)
        f_wait(p, below, 7)
        half = held(p, y_at(-1), x_hi, True, 0)
        f_put(p, half, half, 9, y_up)
        f_put(p, below, below, 12, x_far)
        f_wait(p, above, 8)
        half = held(p, y_at(1), x_hi, True, 1)
        f_put(p, half, half, 10, y_down)
        f_put(p, above, above, 13, x_far)

    def factors_third(p):
        below = held(p, y_at(-1), x_hi, False)
        f_wait(p, below, 1)
        f_put(p, below, below, 5, y_up)
        above = held(p, y_at(1), 1 - x_hi, False)
        f_wait(p, above, 4)
        f_put(p, above, above, 6, y_down)
        for half in range(2):
            f_wait(p, held(p, y_at(2), x_hi, True, half), 9 + half)
        opposite = held(p, y_at(2), x_hi, True)
        f_put(p, opposite, opposite, 14, x_far)

    def factors_end(p):
        f_wait(p, held(p, y_at(1), x_hi, False), 2)
        f_wait(p, held(p, y_at(-1), 1 - x_hi, False), 3)
        f_wait(p, held(p, y_at(2), x_hi, False), 5)
        f_wait(p, held(p, y_at(2), 1 - x_hi, False), 6)
        for at, step in ((11, 0), (12, -1), (13, 1), (14, 2)):
            f_wait(p, held(p, y_at(step), 1 - x_hi, True), at)
        own_copy(p).wait()

    def unit(level, part):
        return level * PARTS + part

    def update(lower, upper, part, a):
        p, source = pair_of(lower, upper), solved[unit(lower, part)]
        total = jnp.zeros((CHUNK, BLK), jnp.float32)
        for group in range(FAN // 2):
            picked = [source[owner[lower, pattern[p, a, group * 2 + q]]] for q in range(2)]
            blocks = [factors[p, group, a, q] for q in range(2)]
            total += transposed_product(jnp.concatenate(picked, axis=1), jnp.concatenate(blocks, axis=1))
        return total

    def later(lower, upper, part):
        def body(a, _):
            product = update(lower, upper, part, a)
            if lower > 0:
                product += pending[upper, part, a]
            pending[upper, part, a] = product
            return 0

        lax.fori_loop(0, OWN, body, 0)

    def solve(level, part):
        def body(a, _):
            residue = rhs_t[level, a, pl.ds(part * CHUNK, CHUNK)]
            if level > 0:
                updates = update(level - 1, level, part, a)
                if level > 1:
                    updates += pending[level, part, a]
                residue = (residue.astype(jnp.float32) - updates).astype(jnp.bfloat16)
            result = transposed_product(residue, diag[level, a]).astype(jnp.bfloat16)
            if level < LEVELS - 1:
                solved[unit(level, part)][leaf * OWN + a] = result
            else:
                last[a, pl.ds(part * CHUNK, CHUNK)] = result
            return 0

        lax.fori_loop(0, OWN, body, 0)

    def turn(level):
        for a in range(OWN):
            rhs_t[level, a] = right_side[level, a].T

    def write(level):
        for a in range(OWN):
            if level < LEVELS - 1:
                parts = [solved[unit(level, part)][leaf * OWN + a] for part in range(PARTS)]
                block = jnp.concatenate(parts, axis=0)
            else:
                block = last[a]
            out[level, a] = block.T

    barrier = pltpu.get_barrier_semaphore()
    for device in partners:
        pl.semaphore_signal(barrier, inc=1, device_id=device, device_id_type=MESH)
    turn(0)
    solve(0, 0)
    solve(0, 1)
    pl.semaphore_wait(barrier, len(partners))

    PER, LAG, EVERY, SECOND, THIRD = 7, 3, 4, 3, 6
    done = set()

    def need(p):
        if p not in done:
            done.add(p)
            factors_end(p)

    def chain(part, at):
        if at < 0 or at >= 3 * PER:
            return
        level, step = divmod(at, PER)
        u = unit(level, part)
        if step == 0:
            if level > 0:
                need(pair_of(level - 1, level))
                solve(level, part)
            gather_start(u)
        elif step <= 5:
            gather_step(u, step - 1)
            if step == 3 and level == 1:
                need(pair_of(0, 2))
                later(0, 2, part)
            if step == 5 and level == 2:
                need(pair_of(0, 3))
                later(0, 3, part)
        else:
            gather_end(u)

    for tick in range(3 * PER + LAG + 8):
        for i, p in enumerate(PAIR_ORDER):
            if tick == EVERY * i + SECOND:
                factors_second(p)
            if tick == EVERY * i + THIRD:
                factors_third(p)
        chain(0, tick)
        for i, p in enumerate(PAIR_ORDER):
            if tick == EVERY * i:
                factors_send(p)
        chain(1, tick - LAG)
        if tick == 4:
            for level in range(1, LEVELS):
                turn(level)
    need(pair_of(1, 3))
    for part in range(PARTS):
        later(1, 3, part)
    for level in range(LEVELS - 1):
        write(level)
    need(pair_of(2, 3))
    for part in range(PARTS):
        solve(3, part)
    write(3)
    for copy in sends:
        copy.wait_send()


def per_device(right_side, diag_inverse, factors, pattern, owner_map):
    vmem = pl.BlockSpec(memory_space=pltpu.VMEM)
    smem = pl.BlockSpec(memory_space=pltpu.SMEM)
    return pl.pallas_call(
        kernel,
        out_shape=jax.ShapeDtypeStruct(right_side.shape, jnp.bfloat16),
        in_specs=[smem, smem, vmem, vmem, pl.BlockSpec(memory_space=pl.ANY)],
        out_specs=vmem,
        scratch_shapes=[pltpu.VMEM((SUPS, CHUNK, BLK), jnp.bfloat16)] * (3 * PARTS)
        + [
            pltpu.VMEM((PAIRS, FAN // 2, OWN, 2, BLK, BLK), jnp.bfloat16),
            pltpu.VMEM((LEVELS, PARTS, OWN, CHUNK, BLK), jnp.float32),
            pltpu.VMEM((LEVELS, OWN, COLS, BLK), jnp.bfloat16),
            pltpu.VMEM((OWN, COLS, BLK), jnp.bfloat16),
            pltpu.SemaphoreType.DMA((3 * PARTS, GATHER_SEMS)),
            pltpu.SemaphoreType.DMA((3 * PARTS, GATHER_SEMS)),
            pltpu.SemaphoreType.DMA((PAIRS, FACTOR_SEMS)),
            pltpu.SemaphoreType.DMA((PAIRS, FACTOR_SEMS)),
            pltpu.SemaphoreType.DMA((PAIRS,)),
        ],
        compiler_params=pltpu.CompilerParams(collective_id=0, has_side_effects=True, vmem_limit_bytes=48 << 20),
        name="substitution",
    )(pattern, owner_map, right_side, diag_inverse, factors)


def solution(mesh):
    return jax.shard_map(
        per_device,
        mesh=mesh,
        in_specs=(
            P(None, "leaf", None, "launch"),
            P(None, "leaf", None, None),
            P(None, "leaf", "launch", None, None),
            P(None, "leaf", None),
            P(),
        ),
        out_specs=P(None, "leaf", None, "launch"),
        check_vma=False,
    )
```

```python
import jax
import jax.numpy as jnp
from jax import lax
from jax.experimental import pallas as pl
from jax.experimental.pallas import tpu as pltpu
from jax.sharding import PartitionSpec as P

LEVELS = 4
FAN = 16
SUPS = 128
OWN = 4
BLK = 128
COLS = 128
PARTS = 2
CHUNK = COLS // PARTS
PAIRS = 6
ZS = 8
YS = 4
LEAFS = 16

X_FIRST = (2, 2, 3, 3, 3, 2)

STEPS = (
    (5,0,2), (0,0,0), (5,1,2), (0,0,1), (5,0,0), (5,3,2), (1,0,0), (5,0,1), (5,3,0), (7,0,1), (7,0,0), (2,0,1,0,0,1),
    (2,0,0,0,1,1), (5,0,3), (2,0,0,0,0,1), (5,3,1), (2,0,0,1,0,1), (2,0,0,1,1,1), (1,0,1), (5,4,3), (2,0,1,0,1,1),
    (2,0,0,0,0,2), (2,0,0,1,0,2), (2,0,1,1,0,1), (9,0), (6,0), (5,4,1), (2,0,0,1,1,2), (2,0,1,1,1,1), (2,0,0,0,1,2),
    (2,0,1,0,1,2), (2,0,0,1,1,3), (8,0,0), (7,3,0), (2,0,0,0,0,3), (2,0,1,1,0,2), (8,0,1), (2,0,1,1,1,2),
    (2,0,0,1,0,3), (5,1,1), (2,0,1,0,0,2), (5,2,0), (7,3,1), (2,0,0,0,1,3), (2,0,1,1,1,3), (2,0,1,1,0,3), (3,0,0,0),
    (5,4,2), (2,0,1,0,0,3), (3,0,0,1), (6,3), (5,5,2), (5,2,2), (2,0,1,0,1,3), (0,1,0), (5,1,0), (3,0,1,1), (3,0,1,0),
    (0,1,1), (2,1,0,0,0,1), (1,1,0), (2,1,0,0,1,1), (5,4,0), (7,1,1), (2,1,1,0,1,1), (1,1,1), (2,1,1,0,0,1), (5,5,1),
    (2,1,0,1,0,1), (5,1,3), (6,1), (2,1,0,1,1,1), (7,1,0), (2,1,1,1,0,1), (8,3,1), (2,1,1,0,0,2), (2,1,1,1,1,1),
    (2,1,0,0,1,2), (2,1,0,1,1,2), (8,3,0), (2,1,0,1,0,2), (9,3), (2,1,1,1,0,2), (2,1,1,0,1,2), (9,1), (8,1,1),
    (2,1,0,0,0,2), (2,1,1,0,0,3), (7,4,0), (2,1,1,1,1,2), (5,3,3), (5,5,0), (8,1,0), (2,1,0,1,1,3), (2,1,0,0,1,3),
    (6,2), (7,4,1), (2,1,0,1,0,3), (5,2,1), (2,1,1,1,0,3), (6,4), (2,1,0,0,0,3), (2,1,1,0,1,3), (3,1,0,1),
    (2,1,1,1,1,3), (4,0,2,1), (3,1,0,0), (4,0,2,0), (3,1,1,0), (0,2,0), (5,2,3), (3,1,1,1), (0,2,1), (7,2,0), (1,2,0),
    (7,5,0), (2,2,0,0,0,1), (2,2,0,0,1,1), (7,2,1), (6,5), (7,5,1), (8,2,1), (1,2,1), (2,2,1,0,0,1), (8,2,0),
    (2,2,1,0,1,1), (9,4), (2,2,0,1,0,1), (8,4,1), (2,2,0,0,1,2), (2,2,1,1,0,1), (2,2,1,1,1,1), (2,2,0,1,1,1),
    (2,2,1,0,0,2), (2,2,1,0,1,2), (9,2), (9,5), (2,2,0,1,0,2), (8,4,0), (2,2,1,1,0,2), (2,2,1,1,1,2), (5,5,3),
    (2,2,0,0,0,2), (8,5,1), (2,2,0,1,1,2), (2,2,1,0,1,3), (2,2,1,0,0,3), (8,5,0), (4,0,3,0), (2,2,1,1,0,3),
    (2,2,1,1,1,3), (2,2,0,0,1,3), (2,2,0,1,0,3), (4,0,3,1), (2,2,0,1,1,3), (2,2,0,0,0,3), (4,1,3,0), (3,2,1,0),
    (3,2,1,1), (4,1,3,1), (3,2,0,1), (3,2,0,0), (0,3,1), (0,3,0),
)

GATHER_SEMS = 33
FACTOR_SEMS = 15
MESH = pl.DeviceIdType.MESH


def pair_of(lower, upper):
    return lower * (2 * LEVELS - lower - 1) // 2 + upper - lower - 1


def transposed_product(rows, blocks):
    return lax.dot_general(rows, blocks, (((1,), (1,)), ((), ())), preferred_element_type=jnp.float32)


def kernel(*refs):
    pattern_in, owner_in, right_side_in, diag_in, own_factors, out = refs[:6]
    solved = refs[6 : 6 + 3 * PARTS]
    (factors, pending, rhs_t, last, pattern, owner, right_side, diag, g_send, g_recv, f_send, f_recv, own_sem, in_sem) = (
        refs[6 + 3 * PARTS :]
    )

    leaf = lax.axis_index("leaf")
    launch = lax.axis_index("launch")
    core, z, x_lo = leaf % 2, (leaf // 2) % ZS, leaf // LEAFS
    y, x_hi = launch // 2, launch % 2

    def leaf_at(xl, zz, k):
        return xl * LEAFS + zz * 2 + k

    def z_at(step):
        return (z + step + ZS) % ZS

    def y_at(step):
        return (y + step + YS) % YS

    z_up = (leaf_at(x_lo, z_at(1), core), launch)
    z_down = (leaf_at(x_lo, z_at(-1), core), launch)
    x_near = (leaf_at(1 - x_lo, z, core), launch)
    sibling = (leaf_at(x_lo, z, 1 - core), launch)
    x_far = (leaf, y * 2 + (1 - x_hi))
    y_up = (leaf, y_at(1) * 2 + x_hi)
    y_down = (leaf, y_at(-1) * 2 + x_hi)
    partners = (z_up, z_down, x_near, sibling, x_far, y_up, y_down)

    sends = []

    def send(src, dst, send_sem, recv_sem, device):
        copy = pltpu.make_async_remote_copy(
            src_ref=src, dst_ref=dst, send_sem=send_sem, recv_sem=recv_sem, device_id=device, device_id_type=MESH
        )
        copy.start()
        sends.append(copy)

    def arrived(dst, recv_sem, send_sem):
        pltpu.make_async_remote_copy(
            src_ref=dst, dst_ref=dst, send_sem=send_sem, recv_sem=recv_sem, device_id=sibling, device_id_type=MESH
        ).wait_recv()

    def slots(u, xl, zz, k, half=None):
        first = leaf_at(xl, zz, k) * OWN
        if half is None:
            return solved[u].at[pl.ds(first, OWN)]
        return solved[u].at[pl.ds(first + half * (OWN // 2), OWN // 2)]

    def g_put(u, ref, at, device):
        send(ref, ref, g_send.at[u, at], g_recv.at[u, at], device)

    def g_wait(u, ref, at):
        arrived(ref, g_recv.at[u, at], g_send.at[u, at])

    columns = (x_lo, 1 - x_lo)

    def ring(stream, down, step):
        return 1 + stream * 8 + down * 4 + step - 1

    def side(stream, offset):
        return 17 + stream * 8 + offset % ZS

    def spread(u, stream):
        block = slots(u, columns[stream], z, core)
        g_put(u, block, ring(stream, 0, 1), z_up)
        g_put(u, block, ring(stream, 1, 1), z_down)
        g_put(u, block, side(stream, 0), sibling)

    def gather_start(u):
        g_put(u, slots(u, x_lo, z, core), 0, x_near)
        spread(u, 0)

    def gather_near(u):
        g_wait(u, slots(u, 1 - x_lo, z, core), 0)
        spread(u, 1)

    def gather_ring(u, stream, down, hop):
        xl, offset = columns[stream], hop if down else -hop
        block = slots(u, xl, z_at(offset), core)
        g_wait(u, block, ring(stream, down, hop))
        onward = block if hop < 3 else slots(u, xl, z_at(offset), core, down)
        g_put(u, onward, ring(stream, down, hop + 1), z_down if down else z_up)
        g_put(u, block, side(stream, offset), sibling)

    def gather_last(u, stream):
        xl = columns[stream]
        for down in range(2):
            g_wait(u, slots(u, xl, z_at(4), core, down), ring(stream, down, 4))
        g_put(u, slots(u, xl, z_at(4), core), side(stream, 4), sibling)

    def gather_end(u):
        for stream in range(2):
            for offset in range(ZS):
                g_wait(u, slots(u, columns[stream], z_at(offset), 1 - core), side(stream, offset))

    def held(p, yy, xh, y_first, half=None):
        cut = X_FIRST[p]
        which = pl.ds(cut, OWN - cut) if y_first else pl.ds(0, cut)
        if half is None:
            return factors.at[p, yy * 2 + xh, which]
        return factors.at[p, yy * 2 + xh, which, pl.ds(half, 1)]

    def f_put(p, src, dst, at, device):
        send(src, dst, f_send.at[p, at], f_recv.at[p, at], device)

    def f_wait(p, ref, at):
        arrived(ref, f_recv.at[p, at], f_send.at[p, at])

    def own_copy(p):
        return pltpu.make_async_copy(own_factors.at[p], factors.at[p, launch], own_sem.at[p])

    def factors_send(p, stage):
        cut = X_FIRST[p]
        src_x, src_y = own_factors.at[p, pl.ds(0, cut)], own_factors.at[p, pl.ds(cut, OWN - cut)]
        dst_x, dst_y = held(p, y, x_hi, False), held(p, y, x_hi, True)
        if stage == 0:
            f_put(p, src_x, dst_x, 0, x_far)
            own_copy(p).start()
        elif stage == 1:
            f_put(p, src_x, dst_x, 1, y_up)
            f_put(p, src_x, dst_x, 2, y_down)
        elif stage == 2:
            f_put(p, src_y, dst_y, 7, y_up)
            f_put(p, src_y, dst_y, 8, y_down)
        else:
            f_put(p, src_y, dst_y, 11, x_far)

    def factors_far(p):
        far = held(p, y, 1 - x_hi, False)
        f_wait(p, far, 0)
        f_put(p, far, far, 3, y_up)
        f_put(p, far, far, 4, y_down)

    def factors_onward(p, down):
        step = 1 if down else -1
        block = held(p, y_at(step), x_hi, True)
        f_wait(p, block, 7 + down)
        half = held(p, y_at(step), x_hi, True, down)
        f_put(p, half, half, 9 + down, y_down if down else y_up)
        f_put(p, block, block, 12 + down, x_far)

    def factors_around(p, down):
        block = held(p, y_at(1), 1 - x_hi, False) if down else held(p, y_at(-1), x_hi, False)
        f_wait(p, block, 4 if down else 1)
        f_put(p, block, block, 5 + down, y_down if down else y_up)

    def factors_last(p):
        for half in range(2):
            f_wait(p, held(p, y_at(2), x_hi, True, half), 9 + half)
        opposite = held(p, y_at(2), x_hi, True)
        f_put(p, opposite, opposite, 14, x_far)

    def factors_end(p):
        f_wait(p, held(p, y_at(1), x_hi, False), 2)
        f_wait(p, held(p, y_at(-1), 1 - x_hi, False), 3)
        f_wait(p, held(p, y_at(2), x_hi, False), 5)
        f_wait(p, held(p, y_at(2), 1 - x_hi, False), 6)
        for at, step in ((11, 0), (12, -1), (13, 1), (14, 2)):
            f_wait(p, held(p, y_at(step), 1 - x_hi, True), at)
        own_copy(p).wait()

    def unit(level, part):
        return level * PARTS + part

    def update(lower, upper, part, a):
        p, source = pair_of(lower, upper), solved[unit(lower, part)]
        total = jnp.zeros((CHUNK, BLK), jnp.float32)
        for group in range(FAN // 2):
            picked = [source[owner[lower, pattern[p, a, group * 2 + q]]] for q in range(2)]
            blocks = [factors[p, group, a, q] for q in range(2)]
            total += transposed_product(jnp.concatenate(picked, axis=1), jnp.concatenate(blocks, axis=1))
        return total

    def later(lower, upper, part):
        def body(a, _):
            product = update(lower, upper, part, a)
            if lower > 0:
                product += pending[upper, part, a]
            pending[upper, part, a] = product
            return 0

        lax.fori_loop(0, OWN, body, 0, unroll=True)

    def solve(level, part):
        def body(a, _):
            residue = rhs_t[level, a, pl.ds(part * CHUNK, CHUNK)]
            if level > 0:
                updates = update(level - 1, level, part, a)
                if level > 1:
                    updates += pending[level, part, a]
                residue = (residue.astype(jnp.float32) - updates).astype(jnp.bfloat16)
            result = transposed_product(residue, diag[level, a]).astype(jnp.bfloat16)
            if level < LEVELS - 1:
                solved[unit(level, part)][leaf * OWN + a] = result
            else:
                last[a, pl.ds(part * CHUNK, CHUNK)] = result
            return 0

        lax.fori_loop(0, OWN, body, 0, unroll=True)

    def turn(level):
        for a in range(OWN):
            rhs_t[level, a] = right_side[level, a].T

    def write(level):
        for a in range(OWN):
            if level < LEVELS - 1:
                parts = [solved[unit(level, part)][leaf * OWN + a] for part in range(PARTS)]
                block = jnp.concatenate(parts, axis=0)
            else:
                block = last[a]
            out[level, a] = block.T

    barrier = pltpu.get_barrier_semaphore()
    for device in partners:
        pl.semaphore_signal(barrier, inc=1, device_id=device, device_id_type=MESH)
    loads = [
        pltpu.make_async_copy(src.at[part], dst.at[part], in_sem.at[at, part])
        for part in range(LEVELS)
        for at, (src, dst) in enumerate(((right_side_in, right_side), (diag_in, diag)))
    ]
    tables = [
        pltpu.make_async_copy(src, dst, in_sem.at[2, at])
        for at, (src, dst) in enumerate(((pattern_in, pattern), (owner_in, owner)))
    ]
    for copy in loads + tables:
        copy.start()
    for copy in loads[:2]:
        copy.wait()
    turn(0)
    for part in range(PARTS):
        solve(0, part)
    pl.semaphore_wait(barrier, len(partners))

    waited = set()

    def have_factors(p):
        if p not in waited:
            waited.add(p)
            factors_end(p)

    def have_solved(u):
        if ("s", u) not in waited:
            waited.add(("s", u))
            gather_end(u)

    def step_of(kind, *at):
        if kind == 0:
            level, part = at
            if level > 0:
                if "rest" not in waited:
                    waited.add("rest")
                    for copy in loads[2:] + tables:
                        copy.wait()
                    for other in range(1, LEVELS):
                        turn(other)
                have_solved(unit(level - 1, part))
                have_factors(pair_of(level - 1, level))
                solve(level, part)
            if level < LEVELS - 1:
                gather_start(unit(level, part))
        elif kind == 1:
            gather_near(unit(*at))
        elif kind == 2:
            gather_ring(unit(at[0], at[1]), *at[2:])
        elif kind == 3:
            gather_last(unit(at[0], at[1]), at[2])
        elif kind == 4:
            lower, upper, part = at
            have_solved(unit(lower, part))
            have_factors(pair_of(lower, upper))
            later(lower, upper, part)
        else:
            (factors_send, factors_far, factors_onward, factors_around, factors_last)[kind - 5](*at)

    for step in STEPS:
        if step[:2] == (0, LEVELS - 1) and "out" not in waited:
            waited.add("out")
            for level in range(LEVELS - 1):
                write(level)
        step_of(*step)
    write(LEVELS - 1)
    for copy in sends:
        copy.wait_send()


def per_device(right_side, diag_inverse, factors, pattern, owner_map):
    vmem = pl.BlockSpec(memory_space=pltpu.VMEM)
    anywhere = pl.BlockSpec(memory_space=pl.ANY)
    return pl.pallas_call(
        kernel,
        out_shape=jax.ShapeDtypeStruct(right_side.shape, jnp.bfloat16),
        in_specs=[anywhere] * 5,
        out_specs=vmem,
        scratch_shapes=[pltpu.VMEM((SUPS, CHUNK, BLK), jnp.bfloat16)] * (3 * PARTS)
        + [
            pltpu.VMEM((PAIRS, FAN // 2, OWN, 2, BLK, BLK), jnp.bfloat16),
            pltpu.VMEM((LEVELS, PARTS, OWN, CHUNK, BLK), jnp.float32),
            pltpu.VMEM((LEVELS, OWN, COLS, BLK), jnp.bfloat16),
            pltpu.VMEM((OWN, COLS, BLK), jnp.bfloat16),
            pltpu.SMEM(pattern.shape, jnp.int32),
            pltpu.SMEM(owner_map.shape, jnp.int32),
            pltpu.VMEM(right_side.shape, jnp.bfloat16),
            pltpu.VMEM(diag_inverse.shape, jnp.bfloat16),
            pltpu.SemaphoreType.DMA((3 * PARTS, GATHER_SEMS)),
            pltpu.SemaphoreType.DMA((3 * PARTS, GATHER_SEMS)),
            pltpu.SemaphoreType.DMA((PAIRS, FACTOR_SEMS)),
            pltpu.SemaphoreType.DMA((PAIRS, FACTOR_SEMS)),
            pltpu.SemaphoreType.DMA((PAIRS,)),
            pltpu.SemaphoreType.DMA((3, LEVELS)),
        ],
        compiler_params=pltpu.CompilerParams(collective_id=0, has_side_effects=True, vmem_limit_bytes=62 << 20),
        name="substitution",
    )(pattern, owner_map, right_side, diag_inverse, factors)


def solution(mesh):
    return jax.shard_map(
        per_device,
        mesh=mesh,
        in_specs=(
            P(None, "leaf", None, "launch"),
            P(None, "leaf", None, None),
            P(None, "leaf", "launch", None, None),
            P(None, "leaf", None),
            P(),
        ),
        out_specs=P(None, "leaf", None, "launch"),
        check_vma=False,
    )
```

```python
import jax
import jax.numpy as jnp
from jax import lax
from jax.experimental import pallas as pl
from jax.experimental.pallas import tpu as pltpu
from jax.sharding import PartitionSpec as P

LEVELS = 4
FAN = 16
SUPS = 128
OWN = 4
BLK = 128
COLS = 128
PARTS = 2
CHUNK = COLS // PARTS
PAIRS = 6
ZS = 8
YS = 4
LEAFS = 16

X_FIRST = (2, 2, 3, 3, 3, 2)

STEPS = (
    (5,0,2), (0,0,0), (5,1,2), (0,0,1), (5,0,0), (5,3,2), (1,0,0), (5,0,1), (5,3,0), (7,0,1), (7,0,0), (2,0,1,0,0,1),
    (2,0,0,0,1,1), (5,0,3), (2,0,0,0,0,1), (5,3,1), (2,0,0,1,0,1), (2,0,0,1,1,1), (1,0,1), (5,4,3), (2,0,1,0,1,1),
    (2,0,0,0,0,2), (2,0,0,1,0,2), (2,0,1,1,0,1), (9,0), (6,0), (5,4,1), (2,0,0,1,1,2), (2,0,1,1,1,1), (2,0,0,0,1,2),
    (2,0,1,0,1,2), (2,0,0,1,1,3), (8,0,0), (7,3,0), (2,0,0,0,0,3), (2,0,1,1,0,2), (8,0,1), (2,0,1,1,1,2),
    (2,0,0,1,0,3), (5,1,1), (2,0,1,0,0,2), (5,2,0), (7,3,1), (2,0,0,0,1,3), (2,0,1,1,1,3), (2,0,1,1,0,3), (3,0,0,0),
    (5,4,2), (2,0,1,0,0,3), (3,0,0,1), (6,3), (5,5,2), (5,2,2), (2,0,1,0,1,3), (0,1,0), (5,1,0), (3,0,1,1), (3,0,1,0),
    (0,1,1), (2,1,0,0,0,1), (1,1,0), (2,1,0,0,1,1), (5,4,0), (7,1,1), (2,1,1,0,1,1), (1,1,1), (2,1,1,0,0,1), (5,5,1),
    (2,1,0,1,0,1), (5,1,3), (6,1), (2,1,0,1,1,1), (7,1,0), (2,1,1,1,0,1), (8,3,1), (2,1,1,0,0,2), (2,1,1,1,1,1),
    (2,1,0,0,1,2), (2,1,0,1,1,2), (8,3,0), (2,1,0,1,0,2), (9,3), (2,1,1,1,0,2), (2,1,1,0,1,2), (9,1), (8,1,1),
    (2,1,0,0,0,2), (2,1,1,0,0,3), (7,4,0), (2,1,1,1,1,2), (5,3,3), (5,5,0), (8,1,0), (2,1,0,1,1,3), (2,1,0,0,1,3),
    (6,2), (7,4,1), (2,1,0,1,0,3), (5,2,1), (2,1,1,1,0,3), (6,4), (2,1,0,0,0,3), (2,1,1,0,1,3), (3,1,0,1),
    (2,1,1,1,1,3), (4,0,2,1), (3,1,0,0), (4,0,2,0), (3,1,1,0), (0,2,0), (5,2,3), (3,1,1,1), (0,2,1), (7,2,0), (1,2,0),
    (7,5,0), (2,2,0,0,0,1), (2,2,0,0,1,1), (7,2,1), (6,5), (7,5,1), (8,2,1), (1,2,1), (2,2,1,0,0,1), (8,2,0),
    (2,2,1,0,1,1), (9,4), (2,2,0,1,0,1), (8,4,1), (2,2,0,0,1,2), (2,2,1,1,0,1), (2,2,1,1,1,1), (2,2,0,1,1,1),
    (2,2,1,0,0,2), (2,2,1,0,1,2), (9,2), (9,5), (2,2,0,1,0,2), (8,4,0), (2,2,1,1,0,2), (2,2,1,1,1,2), (5,5,3),
    (2,2,0,0,0,2), (8,5,1), (2,2,0,1,1,2), (2,2,1,0,1,3), (2,2,1,0,0,3), (8,5,0), (4,0,3,0), (2,2,1,1,0,3),
    (2,2,1,1,1,3), (2,2,0,0,1,3), (2,2,0,1,0,3), (4,0,3,1), (2,2,0,1,1,3), (2,2,0,0,0,3), (4,1,3,0), (3,2,1,0),
    (3,2,1,1), (4,1,3,1), (3,2,0,1), (3,2,0,0), (0,3,1), (0,3,0),
)

GATHER_SEMS = 16
LINE, SIDE = 13, 15
FACTOR_SEM = {0: 0, 1: 1, 4: 2, 7: 3, 8: 4, 9: 5, 10: 5}
FACTOR_END = 6
MESH = pl.DeviceIdType.MESH


def pair_of(lower, upper):
    return lower * (2 * LEVELS - lower - 1) // 2 + upper - lower - 1


def transposed_product(rows, blocks):
    return lax.dot_general(rows, blocks, (((1,), (1,)), ((), ())), preferred_element_type=jnp.float32)


def kernel(*refs):
    pattern_in, owner_in, right_side_in, diag_in, own_factors, out = refs[:6]
    solved = refs[6 : 6 + 3 * PARTS]
    (factors, pending, rhs_t, last, pattern, owner, right_side, diag, g_send, g_recv, f_send, f_recv, own_sem, in_sem) = (
        refs[6 + 3 * PARTS :]
    )

    leaf = lax.axis_index("leaf")
    launch = lax.axis_index("launch")
    core, z, x_lo = leaf % 2, (leaf // 2) % ZS, leaf // LEAFS
    y, x_hi = launch // 2, launch % 2

    def leaf_at(xl, zz, k):
        return xl * LEAFS + zz * 2 + k

    def z_at(step):
        return (z + step + ZS) % ZS

    def y_at(step):
        return (y + step + YS) % YS

    z_up = (leaf_at(x_lo, z_at(1), core), launch)
    z_down = (leaf_at(x_lo, z_at(-1), core), launch)
    x_near = (leaf_at(1 - x_lo, z, core), launch)
    sibling = (leaf_at(x_lo, z, 1 - core), launch)
    x_far = (leaf, y * 2 + (1 - x_hi))
    y_up = (leaf, y_at(1) * 2 + x_hi)
    y_down = (leaf, y_at(-1) * 2 + x_hi)
    partners = (z_up, z_down, x_near, sibling, x_far, y_up, y_down)

    def send(src, dst, send_sem, recv_sem, device):
        copy = pltpu.make_async_remote_copy(
            src_ref=src, dst_ref=dst, send_sem=send_sem, recv_sem=recv_sem, device_id=device, device_id_type=MESH
        )
        copy.start()

    def arrived(dst, recv_sem, send_sem):
        pltpu.make_async_remote_copy(
            src_ref=dst, dst_ref=dst, send_sem=send_sem, recv_sem=recv_sem, device_id=sibling, device_id_type=MESH
        ).wait_recv()

    def slots(u, xl, zz, k, half=None):
        first = leaf_at(xl, zz, k) * OWN
        if half is None:
            return solved[u].at[pl.ds(first, OWN)]
        return solved[u].at[pl.ds(first + half * (OWN // 2), OWN // 2)]

    def g_put(u, ref, at, device):
        send(ref, ref, g_send.at[u], g_recv.at[u, at], device)

    def g_wait(u, ref, at):
        arrived(ref, g_recv.at[u, at], g_send.at[u])

    columns = (x_lo, 1 - x_lo)

    def ring(stream, down, step):
        return LINE + stream if step == 4 else 1 + stream * 6 + down * 3 + step - 1

    def spread(u, stream):
        block = slots(u, columns[stream], z, core)
        g_put(u, block, ring(stream, 0, 1), z_up)
        g_put(u, block, ring(stream, 1, 1), z_down)
        g_put(u, block, SIDE, sibling)

    def gather_start(u):
        g_put(u, slots(u, x_lo, z, core), 0, x_near)
        spread(u, 0)

    def gather_near(u):
        g_wait(u, slots(u, 1 - x_lo, z, core), 0)
        spread(u, 1)

    def gather_ring(u, stream, down, hop):
        xl, offset = columns[stream], hop if down else -hop
        block = slots(u, xl, z_at(offset), core)
        g_wait(u, block, ring(stream, down, hop))
        onward = block if hop < 3 else slots(u, xl, z_at(offset), core, down)
        g_put(u, onward, ring(stream, down, hop + 1), z_down if down else z_up)
        g_put(u, block, SIDE, sibling)

    def gather_last(u, stream):
        xl = columns[stream]
        g_wait(u, slots(u, xl, z_at(4), core), LINE + stream)
        g_put(u, slots(u, xl, z_at(4), core), SIDE, sibling)

    def gather_end(u):
        g_wait(u, solved[u].at[pl.ds(0, SUPS // 2)], SIDE)

    def gather_sent(u):
        ref = solved[u].at[pl.ds(0, OWN * (1 + 2 * (ZS - 1)) + SUPS // 2)]
        pltpu.make_async_remote_copy(
            src_ref=ref, dst_ref=ref, send_sem=g_send.at[u], recv_sem=g_recv.at[u, 0],
            device_id=sibling, device_id_type=MESH,
        ).wait_send()

    def held(p, yy, xh, y_first, half=None):
        cut = X_FIRST[p]
        which = pl.ds(cut, OWN - cut) if y_first else pl.ds(0, cut)
        if half is None:
            return factors.at[p, yy * 2 + xh, which]
        return factors.at[p, yy * 2 + xh, which, pl.ds(half, 1)]

    def f_put(p, src, dst, at, device):
        send(src, dst, f_send.at[p], f_recv.at[p, FACTOR_SEM.get(at, FACTOR_END)], device)

    def f_wait(p, ref, at):
        arrived(ref, f_recv.at[p, FACTOR_SEM.get(at, FACTOR_END)], f_send.at[p])

    def own_copy(p):
        return pltpu.make_async_copy(own_factors.at[p], factors.at[p, launch], own_sem.at[p])

    def factors_send(p, stage):
        cut = X_FIRST[p]
        src_x, src_y = own_factors.at[p, pl.ds(0, cut)], own_factors.at[p, pl.ds(cut, OWN - cut)]
        dst_x, dst_y = held(p, y, x_hi, False), held(p, y, x_hi, True)
        if stage == 0:
            f_put(p, src_x, dst_x, 0, x_far)
            own_copy(p).start()
        elif stage == 1:
            f_put(p, src_x, dst_x, 1, y_up)
            f_put(p, src_x, dst_x, 2, y_down)
        elif stage == 2:
            f_put(p, src_y, dst_y, 7, y_up)
            f_put(p, src_y, dst_y, 8, y_down)
        else:
            f_put(p, src_y, dst_y, 11, x_far)

    def factors_far(p):
        far = held(p, y, 1 - x_hi, False)
        f_wait(p, far, 0)
        f_put(p, far, far, 3, y_up)
        f_put(p, far, far, 4, y_down)

    def factors_onward(p, down):
        step = 1 if down else -1
        block = held(p, y_at(step), x_hi, True)
        f_wait(p, block, 7 + down)
        half = held(p, y_at(step), x_hi, True, down)
        f_put(p, half, half, 9 + down, y_down if down else y_up)
        f_put(p, block, block, 12 + down, x_far)

    def factors_around(p, down):
        block = held(p, y_at(1), 1 - x_hi, False) if down else held(p, y_at(-1), x_hi, False)
        f_wait(p, block, 4 if down else 1)
        f_put(p, block, block, 5 + down, y_down if down else y_up)

    def factors_last(p):
        opposite = held(p, y_at(2), x_hi, True)
        f_wait(p, opposite, 9)
        f_put(p, opposite, opposite, 14, x_far)

    def factors_end(p):
        arrived(factors.at[p, pl.ds(0, 4)], f_recv.at[p, FACTOR_END], f_send.at[p])
        own_copy(p).wait()

    def factors_sent(p):
        ref = factors.at[p, pl.ds(0, 7)]
        pltpu.make_async_remote_copy(
            src_ref=ref, dst_ref=ref, send_sem=f_send.at[p], recv_sem=f_recv.at[p, 0],
            device_id=sibling, device_id_type=MESH,
        ).wait_send()

    def unit(level, part):
        return level * PARTS + part

    def update(lower, upper, part, a):
        p, source = pair_of(lower, upper), solved[unit(lower, part)]
        total = jnp.zeros((CHUNK, BLK), jnp.float32)
        for group in range(FAN // 2):
            picked = [source[owner[lower, pattern[p, a, group * 2 + q]]] for q in range(2)]
            blocks = [factors[p, group, a, q] for q in range(2)]
            total += transposed_product(jnp.concatenate(picked, axis=1), jnp.concatenate(blocks, axis=1))
        return total

    def later(lower, upper, part):
        def body(a, _):
            product = update(lower, upper, part, a)
            if lower > 0:
                product += pending[upper, part, a]
            pending[upper, part, a] = product
            return 0

        lax.fori_loop(0, OWN, body, 0, unroll=True)

    def solve(level, part):
        def body(a, _):
            residue = rhs_t[level, a, pl.ds(part * CHUNK, CHUNK)]
            if level > 0:
                updates = update(level - 1, level, part, a)
                if level > 1:
                    updates += pending[level, part, a]
                residue = (residue.astype(jnp.float32) - updates).astype(jnp.bfloat16)
            result = transposed_product(residue, diag[level, a]).astype(jnp.bfloat16)
            if level < LEVELS - 1:
                solved[unit(level, part)][leaf * OWN + a] = result
            else:
                last[a, pl.ds(part * CHUNK, CHUNK)] = result
            return 0

        lax.fori_loop(0, OWN, body, 0, unroll=True)

    def turn(level):
        for a in range(OWN):
            rhs_t[level, a] = right_side[level, a].T

    def write(level):
        for a in range(OWN):
            if level < LEVELS - 1:
                parts = [solved[unit(level, part)][leaf * OWN + a] for part in range(PARTS)]
                block = jnp.concatenate(parts, axis=0)
            else:
                block = last[a]
            out[level, a] = block.T

    barrier = pltpu.get_barrier_semaphore()
    for device in partners:
        pl.semaphore_signal(barrier, inc=1, device_id=device, device_id_type=MESH)
    loads = [
        pltpu.make_async_copy(src.at[levels], dst.at[levels], in_sem.at[at, part])
        for part, levels in enumerate((pl.ds(0, 1), pl.ds(1, LEVELS - 1)))
        for at, (src, dst) in enumerate(((right_side_in, right_side), (diag_in, diag)))
    ]
    tables = [
        pltpu.make_async_copy(src, dst, in_sem.at[2, at])
        for at, (src, dst) in enumerate(((pattern_in, pattern), (owner_in, owner)))
    ]
    for copy in loads + tables:
        copy.start()
    for copy in loads[:2]:
        copy.wait()
    turn(0)
    for part in range(PARTS):
        solve(0, part)
    pl.semaphore_wait(barrier, len(partners))

    waited = set()

    def have_factors(p):
        if p not in waited:
            waited.add(p)
            factors_end(p)

    def have_solved(u):
        if ("s", u) not in waited:
            waited.add(("s", u))
            gather_end(u)

    def step_of(kind, *at):
        if kind == 0:
            level, part = at
            if level > 0:
                if "rest" not in waited:
                    waited.add("rest")
                    for copy in loads[2:] + tables:
                        copy.wait()
                    for other in range(1, LEVELS):
                        turn(other)
                have_solved(unit(level - 1, part))
                have_factors(pair_of(level - 1, level))
                solve(level, part)
            if level < LEVELS - 1:
                gather_start(unit(level, part))
        elif kind == 1:
            gather_near(unit(*at))
        elif kind == 2:
            gather_ring(unit(at[0], at[1]), *at[2:])
        elif kind == 3:
            gather_last(unit(at[0], at[1]), at[2])
        elif kind == 4:
            lower, upper, part = at
            have_solved(unit(lower, part))
            have_factors(pair_of(lower, upper))
            later(lower, upper, part)
        else:
            (factors_send, factors_far, factors_onward, factors_around, factors_last)[kind - 5](*at)

    for step in STEPS:
        if step[:2] == (0, LEVELS - 1) and "out" not in waited:
            waited.add("out")
            for level in range(LEVELS - 1):
                write(level)
        step_of(*step)
    write(LEVELS - 1)
    for u in range(3 * PARTS):
        gather_sent(u)
    for p in range(PAIRS):
        factors_sent(p)


def per_device(right_side, diag_inverse, factors, pattern, owner_map):
    vmem = pl.BlockSpec(memory_space=pltpu.VMEM)
    anywhere = pl.BlockSpec(memory_space=pl.ANY)
    return pl.pallas_call(
        kernel,
        out_shape=jax.ShapeDtypeStruct(right_side.shape, jnp.bfloat16),
        in_specs=[anywhere] * 5,
        out_specs=vmem,
        scratch_shapes=[pltpu.VMEM((SUPS, CHUNK, BLK), jnp.bfloat16)] * (3 * PARTS)
        + [
            pltpu.VMEM((PAIRS, FAN // 2, OWN, 2, BLK, BLK), jnp.bfloat16),
            pltpu.VMEM((LEVELS, PARTS, OWN, CHUNK, BLK), jnp.float32),
            pltpu.VMEM((LEVELS, OWN, COLS, BLK), jnp.bfloat16),
            pltpu.VMEM((OWN, COLS, BLK), jnp.bfloat16),
            pltpu.SMEM(pattern.shape, jnp.int32),
            pltpu.SMEM(owner_map.shape, jnp.int32),
            pltpu.VMEM(right_side.shape, jnp.bfloat16),
            pltpu.VMEM(diag_inverse.shape, jnp.bfloat16),
            pltpu.SemaphoreType.DMA((3 * PARTS,)),
            pltpu.SemaphoreType.DMA((3 * PARTS, GATHER_SEMS)),
            pltpu.SemaphoreType.DMA((PAIRS,)),
            pltpu.SemaphoreType.DMA((PAIRS, FACTOR_END + 1)),
            pltpu.SemaphoreType.DMA((PAIRS,)),
            pltpu.SemaphoreType.DMA((3, 2)),
        ],
        compiler_params=pltpu.CompilerParams(collective_id=0, has_side_effects=True, vmem_limit_bytes=62 << 20),
        name="substitution",
    )(pattern, owner_map, right_side, diag_inverse, factors)


def solution(mesh):
    return jax.shard_map(
        per_device,
        mesh=mesh,
        in_specs=(
            P(None, "leaf", None, "launch"),
            P(None, "leaf", None, None),
            P(None, "leaf", "launch", None, None),
            P(None, "leaf", None),
            P(),
        ),
        out_specs=P(None, "leaf", None, "launch"),
        check_vma=False,
    )
```

```python
import jax
import jax.numpy as jnp
from jax import lax
from jax.experimental import pallas as pl
from jax.experimental.pallas import tpu as pltpu
from jax.sharding import PartitionSpec as P

LEVELS = 4
FAN = 16
SUPS = 128
OWN = 4
BLK = 128
COLS = 128
PARTS = 2
CHUNK = COLS // PARTS
PAIRS = 6
ZS = 8
YS = 4
LEAFS = 16

X_FIRST = (3, 3, 2, 2, 2, 3)

STEPS = (
    (5,0,1), (0,0,0), (5,0,2), (0,0,1), (5,3,2), (5,0,0), (5,1,0), (5,3,0), (5,4,2), (1,0,0), (2,0,0,0,0,1),
    (2,0,0,0,1,1), (1,0,1), (2,0,1,0,1,1), (5,1,2), (2,0,0,1,0,1), (2,0,0,1,1,1), (6,0), (2,0,0,0,0,2), (2,0,0,0,1,2),
    (5,0,3), (7,0,1), (5,4,0), (2,0,1,1,0,1), (7,0,0), (2,0,1,0,0,1), (2,0,1,1,1,1), (7,1,0), (2,0,1,0,1,2),
    (2,0,0,1,1,2), (2,0,0,1,0,2), (7,1,1), (8,0,0), (2,0,0,0,1,3), (2,0,0,0,0,3), (6,3), (2,0,1,1,0,2), (2,0,1,1,1,2),
    (8,0,1), (5,1,1), (2,0,1,0,0,2), (9,0), (7,3,0), (2,0,0,1,0,3), (6,1), (2,0,0,1,1,3), (2,0,1,1,1,3),
    (2,0,1,0,1,3), (2,0,1,1,0,3), (2,0,1,0,0,3), (7,4,0), (3,0,0,1), (3,0,0,0), (0,1,0), (3,0,1,1), (3,0,1,0),
    (0,1,1), (7,3,1), (5,2,2), (9,1), (1,1,0), (1,1,1), (5,3,3), (2,1,1,0,1,1), (2,1,0,0,1,1), (5,3,1), (8,1,1),
    (2,1,0,0,0,1), (2,1,1,0,0,1), (5,1,3), (5,5,0), (2,1,1,1,0,1), (2,1,1,1,1,1), (8,1,0), (5,4,1), (7,4,1), (9,3),
    (5,2,0), (2,1,0,1,0,1), (2,1,0,1,1,1), (2,1,1,0,1,2), (8,3,0), (2,1,1,0,0,2), (2,1,1,1,0,2), (2,1,1,1,1,2),
    (2,1,0,1,0,2), (2,1,0,0,1,2), (8,3,1), (5,5,1), (2,1,0,1,1,2), (2,1,0,0,0,2), (5,5,2), (2,1,1,0,0,3),
    (2,1,1,0,1,3), (4,0,2,0), (2,1,1,1,1,3), (2,1,1,1,0,3), (2,1,0,0,1,3), (2,1,0,1,0,3), (2,1,0,0,0,3),
    (2,1,0,1,1,3), (7,2,1), (5,2,1), (6,4), (3,1,1,0), (3,1,1,1), (4,0,2,1), (0,2,1), (3,1,0,0), (8,4,0), (3,1,0,1),
    (0,2,0), (9,4), (6,5), (1,2,1), (2,2,1,0,0,1), (5,4,3), (2,2,1,0,1,1), (1,2,0), (2,2,0,0,0,1), (7,5,0),
    (2,2,0,0,1,1), (7,2,0), (6,2), (2,2,1,1,0,1), (8,4,1), (2,2,1,1,1,1), (8,2,0), (7,5,1), (2,2,0,1,0,1),
    (2,2,0,1,1,1), (2,2,1,0,1,2), (2,2,0,0,0,2), (2,2,1,1,0,2), (2,2,1,1,1,2), (2,2,0,0,1,2), (5,2,3), (2,2,0,1,0,2),
    (8,2,1), (2,2,0,1,1,2), (9,2), (2,2,1,0,0,2), (2,2,0,0,0,3), (8,5,1), (2,2,1,0,1,3), (8,5,0), (4,1,3,1), (5,5,3),
    (2,2,1,1,1,3), (9,5), (2,2,1,1,0,3), (2,2,0,0,1,3), (4,1,3,0), (2,2,0,1,0,3), (2,2,0,1,1,3), (2,2,1,0,0,3),
    (3,2,0,0), (4,0,3,0), (3,2,1,1), (3,2,0,1), (4,0,3,1), (3,2,1,0), (0,3,0), (0,3,1),
)

GATHER_SEMS = 16
LINE, SIDE = 13, 15
FACTOR_SEM = {0: 0, 1: 1, 4: 2, 7: 3, 8: 4, 9: 5, 10: 5}
FACTOR_END = 6
MESH = pl.DeviceIdType.MESH


def pair_of(lower, upper):
    return lower * (2 * LEVELS - lower - 1) // 2 + upper - lower - 1


def transposed_product(rows, blocks):
    return lax.dot_general(rows, blocks, (((1,), (1,)), ((), ())), preferred_element_type=jnp.float32)


def kernel(*refs):
    pattern_in, owner_in, right_side_in, diag_in, own_factors, out = refs[:6]
    solved = refs[6 : 6 + 3 * PARTS]
    (factors, pending, rhs_t, last, pattern, owner, right_side, diag, g_send, g_recv, f_send, f_recv, own_sem, in_sem) = (
        refs[6 + 3 * PARTS :]
    )

    leaf = lax.axis_index("leaf")
    launch = lax.axis_index("launch")
    core, z, x_lo = leaf % 2, (leaf // 2) % ZS, leaf // LEAFS
    y, x_hi = launch // 2, launch % 2

    def leaf_at(xl, zz, k):
        return xl * LEAFS + zz * 2 + k

    def z_at(step):
        return (z + step + ZS) % ZS

    def y_at(step):
        return (y + step + YS) % YS

    z_up = (leaf_at(x_lo, z_at(1), core), launch)
    z_down = (leaf_at(x_lo, z_at(-1), core), launch)
    x_near = (leaf_at(1 - x_lo, z, core), launch)
    sibling = (leaf_at(x_lo, z, 1 - core), launch)
    x_far = (leaf, y * 2 + (1 - x_hi))
    y_up = (leaf, y_at(1) * 2 + x_hi)
    y_down = (leaf, y_at(-1) * 2 + x_hi)
    partners = (z_up, z_down, x_near, sibling, x_far, y_up, y_down)

    def send(src, dst, send_sem, recv_sem, device):
        copy = pltpu.make_async_remote_copy(
            src_ref=src, dst_ref=dst, send_sem=send_sem, recv_sem=recv_sem, device_id=device, device_id_type=MESH
        )
        copy.start()

    def arrived(dst, recv_sem, send_sem):
        pltpu.make_async_remote_copy(
            src_ref=dst, dst_ref=dst, send_sem=send_sem, recv_sem=recv_sem, device_id=sibling, device_id_type=MESH
        ).wait_recv()

    def slots(u, xl, zz, k, half=None):
        first = leaf_at(xl, zz, k) * OWN
        if half is None:
            return solved[u].at[pl.ds(first, OWN)]
        return solved[u].at[pl.ds(first + half * (OWN // 2), OWN // 2)]

    def g_put(u, ref, at, device):
        send(ref, ref, g_send.at[u], g_recv.at[u, at], device)

    def g_wait(u, ref, at):
        arrived(ref, g_recv.at[u, at], g_send.at[u])

    columns = (x_lo, 1 - x_lo)

    def ring(stream, down, step):
        return LINE + stream if step == 4 else 1 + stream * 6 + down * 3 + step - 1

    def spread(u, stream):
        block = slots(u, columns[stream], z, core)
        g_put(u, block, ring(stream, 0, 1), z_up)
        g_put(u, block, ring(stream, 1, 1), z_down)
        g_put(u, block, SIDE, sibling)

    def gather_start(u):
        g_put(u, slots(u, x_lo, z, core), 0, x_near)
        spread(u, 0)

    def gather_near(u):
        g_wait(u, slots(u, 1 - x_lo, z, core), 0)
        spread(u, 1)

    def gather_ring(u, stream, down, hop):
        xl, offset = columns[stream], hop if down else -hop
        block = slots(u, xl, z_at(offset), core)
        g_wait(u, block, ring(stream, down, hop))
        onward = block if hop < 3 else slots(u, xl, z_at(offset), core, down)
        g_put(u, onward, ring(stream, down, hop + 1), z_down if down else z_up)
        g_put(u, block, SIDE, sibling)

    def gather_last(u, stream):
        xl = columns[stream]
        g_wait(u, slots(u, xl, z_at(4), core), LINE + stream)
        g_put(u, slots(u, xl, z_at(4), core), SIDE, sibling)

    def gather_end(u):
        g_wait(u, solved[u].at[pl.ds(0, SUPS // 2)], SIDE)

    def gather_sent(u):
        ref = solved[u].at[pl.ds(0, OWN * (1 + 2 * (ZS - 1)) + SUPS // 2)]
        pltpu.make_async_remote_copy(
            src_ref=ref, dst_ref=ref, send_sem=g_send.at[u], recv_sem=g_recv.at[u, 0],
            device_id=sibling, device_id_type=MESH,
        ).wait_send()

    def held(p, yy, xh, y_first, half=None):
        cut = X_FIRST[p]
        which = pl.ds(cut, OWN - cut) if y_first else pl.ds(0, cut)
        if half is None:
            return factors.at[p, yy * 2 + xh, which]
        return factors.at[p, yy * 2 + xh, which, pl.ds(half, 1)]

    def f_put(p, src, dst, at, device):
        send(src, dst, f_send.at[p], f_recv.at[p, FACTOR_SEM.get(at, FACTOR_END)], device)

    def f_wait(p, ref, at):
        arrived(ref, f_recv.at[p, FACTOR_SEM.get(at, FACTOR_END)], f_send.at[p])

    def own_copy(p):
        return pltpu.make_async_copy(own_factors.at[p], factors.at[p, launch], own_sem.at[p])

    def factors_send(p, stage):
        cut = X_FIRST[p]
        src_x, src_y = own_factors.at[p, pl.ds(0, cut)], own_factors.at[p, pl.ds(cut, OWN - cut)]
        dst_x, dst_y = held(p, y, x_hi, False), held(p, y, x_hi, True)
        if stage == 0:
            f_put(p, src_x, dst_x, 0, x_far)
            own_copy(p).start()
        elif stage == 1:
            f_put(p, src_x, dst_x, 1, y_up)
            f_put(p, src_x, dst_x, 2, y_down)
        elif stage == 2:
            f_put(p, src_y, dst_y, 7, y_up)
            f_put(p, src_y, dst_y, 8, y_down)
        else:
            f_put(p, src_y, dst_y, 11, x_far)

    def factors_far(p):
        far = held(p, y, 1 - x_hi, False)
        f_wait(p, far, 0)
        f_put(p, far, far, 3, y_up)
        f_put(p, far, far, 4, y_down)

    def factors_onward(p, down):
        step = 1 if down else -1
        block = held(p, y_at(step), x_hi, True)
        f_wait(p, block, 7 + down)
        half = held(p, y_at(step), x_hi, True, down)
        f_put(p, half, half, 9 + down, y_down if down else y_up)
        f_put(p, block, block, 12 + down, x_far)

    def factors_around(p, down):
        block = held(p, y_at(1), 1 - x_hi, False) if down else held(p, y_at(-1), x_hi, False)
        f_wait(p, block, 4 if down else 1)
        f_put(p, block, block, 5 + down, y_down if down else y_up)

    def factors_last(p):
        opposite = held(p, y_at(2), x_hi, True)
        f_wait(p, opposite, 9)
        f_put(p, opposite, opposite, 14, x_far)

    def factors_end(p):
        arrived(factors.at[p, pl.ds(0, 4)], f_recv.at[p, FACTOR_END], f_send.at[p])
        own_copy(p).wait()

    def factors_sent(p):
        ref = factors.at[p, pl.ds(0, 7)]
        pltpu.make_async_remote_copy(
            src_ref=ref, dst_ref=ref, send_sem=f_send.at[p], recv_sem=f_recv.at[p, 0],
            device_id=sibling, device_id_type=MESH,
        ).wait_send()

    def unit(level, part):
        return level * PARTS + part

    def update(lower, upper, part, a):
        p, source = pair_of(lower, upper), solved[unit(lower, part)]
        total = jnp.zeros((CHUNK, BLK), jnp.float32)
        for group in range(FAN // 2):
            picked = [source[owner[lower, pattern[p, a, group * 2 + q]]] for q in range(2)]
            blocks = [factors[p, group, a, q] for q in range(2)]
            total += transposed_product(jnp.concatenate(picked, axis=1), jnp.concatenate(blocks, axis=1))
        return total

    started = set()

    def later(lower, upper, part):
        first = (upper, part) not in started
        started.add((upper, part))

        def body(a, _):
            product = update(lower, upper, part, a)
            if not first:
                product += pending[upper, part, a]
            pending[upper, part, a] = product
            return 0

        lax.fori_loop(0, OWN, body, 0, unroll=True)

    def solve(level, part):
        def body(a, _):
            residue = rhs_t[level, a, pl.ds(part * CHUNK, CHUNK)]
            if level > 0:
                updates = update(level - 1, level, part, a)
                if level > 1:
                    updates += pending[level, part, a]
                residue = (residue.astype(jnp.float32) - updates).astype(jnp.bfloat16)
            result = transposed_product(residue, diag[level, a]).astype(jnp.bfloat16)
            if level < LEVELS - 1:
                solved[unit(level, part)][leaf * OWN + a] = result
            else:
                last[a, pl.ds(part * CHUNK, CHUNK)] = result
            return 0

        lax.fori_loop(0, OWN, body, 0, unroll=True)

    def turn(level):
        for a in range(OWN):
            rhs_t[level, a] = right_side[level, a].T

    def write(level):
        for a in range(OWN):
            if level < LEVELS - 1:
                parts = [solved[unit(level, part)][leaf * OWN + a] for part in range(PARTS)]
                block = jnp.concatenate(parts, axis=0)
            else:
                block = last[a]
            out[level, a] = block.T

    barrier = pltpu.get_barrier_semaphore()
    for device in partners:
        pl.semaphore_signal(barrier, inc=1, device_id=device, device_id_type=MESH)
    loads = [
        pltpu.make_async_copy(src.at[levels], dst.at[levels], in_sem.at[at, part])
        for part, levels in enumerate((pl.ds(0, 1), pl.ds(1, LEVELS - 1)))
        for at, (src, dst) in enumerate(((right_side_in, right_side), (diag_in, diag)))
    ]
    tables = [
        pltpu.make_async_copy(src, dst, in_sem.at[2, at])
        for at, (src, dst) in enumerate(((pattern_in, pattern), (owner_in, owner)))
    ]
    for copy in loads + tables:
        copy.start()
    for copy in loads[:2]:
        copy.wait()
    turn(0)
    for part in range(PARTS):
        solve(0, part)
    pl.semaphore_wait(barrier, len(partners))

    waited = set()

    def have_factors(p):
        if p not in waited:
            waited.add(p)
            factors_end(p)

    def have_solved(u):
        if ("s", u) not in waited:
            waited.add(("s", u))
            gather_end(u)

    def step_of(kind, *at):
        if kind == 0:
            level, part = at
            if level > 0:
                if "rest" not in waited:
                    waited.add("rest")
                    for copy in loads[2:] + tables:
                        copy.wait()
                    for other in range(1, LEVELS):
                        turn(other)
                have_solved(unit(level - 1, part))
                have_factors(pair_of(level - 1, level))
                solve(level, part)
            if level < LEVELS - 1:
                gather_start(unit(level, part))
        elif kind == 1:
            gather_near(unit(*at))
        elif kind == 2:
            gather_ring(unit(at[0], at[1]), *at[2:])
        elif kind == 3:
            gather_last(unit(at[0], at[1]), at[2])
        elif kind == 4:
            lower, upper, part = at
            have_solved(unit(lower, part))
            have_factors(pair_of(lower, upper))
            later(lower, upper, part)
        else:
            (factors_send, factors_far, factors_onward, factors_around, factors_last)[kind - 5](*at)

    for step in STEPS:
        if step[:2] == (0, LEVELS - 1) and "out" not in waited:
            waited.add("out")
            for level in range(LEVELS - 1):
                write(level)
        step_of(*step)
    write(LEVELS - 1)
    for u in range(3 * PARTS):
        gather_sent(u)
    for p in range(PAIRS):
        factors_sent(p)


def per_device(right_side, diag_inverse, factors, pattern, owner_map):
    vmem = pl.BlockSpec(memory_space=pltpu.VMEM)
    anywhere = pl.BlockSpec(memory_space=pl.ANY)
    return pl.pallas_call(
        kernel,
        out_shape=jax.ShapeDtypeStruct(right_side.shape, jnp.bfloat16),
        in_specs=[anywhere] * 5,
        out_specs=vmem,
        scratch_shapes=[pltpu.VMEM((SUPS, CHUNK, BLK), jnp.bfloat16)] * (3 * PARTS)
        + [
            pltpu.VMEM((PAIRS, FAN // 2, OWN, 2, BLK, BLK), jnp.bfloat16),
            pltpu.VMEM((LEVELS, PARTS, OWN, CHUNK, BLK), jnp.float32),
            pltpu.VMEM((LEVELS, OWN, COLS, BLK), jnp.bfloat16),
            pltpu.VMEM((OWN, COLS, BLK), jnp.bfloat16),
            pltpu.SMEM(pattern.shape, jnp.int32),
            pltpu.SMEM(owner_map.shape, jnp.int32),
            pltpu.VMEM(right_side.shape, jnp.bfloat16),
            pltpu.VMEM(diag_inverse.shape, jnp.bfloat16),
            pltpu.SemaphoreType.DMA((3 * PARTS,)),
            pltpu.SemaphoreType.DMA((3 * PARTS, GATHER_SEMS)),
            pltpu.SemaphoreType.DMA((PAIRS,)),
            pltpu.SemaphoreType.DMA((PAIRS, FACTOR_END + 1)),
            pltpu.SemaphoreType.DMA((PAIRS,)),
            pltpu.SemaphoreType.DMA((3, 2)),
        ],
        compiler_params=pltpu.CompilerParams(collective_id=0, has_side_effects=True, vmem_limit_bytes=62 << 20),
        name="substitution",
    )(pattern, owner_map, right_side, diag_inverse, factors)


def solution(mesh):
    return jax.shard_map(
        per_device,
        mesh=mesh,
        in_specs=(
            P(None, "leaf", None, "launch"),
            P(None, "leaf", None, None),
            P(None, "leaf", "launch", None, None),
            P(None, "leaf", None),
            P(),
        ),
        out_specs=P(None, "leaf", None, "launch"),
        check_vma=False,
    )
```
